32 devices in a mesh: gx: 8 (over z, y), gz: 4 (over x, core).
Axes of the slice: x: 2, y: 2, z: 4, core: 2. Of those that a mesh axis runs over, the one named last changes fastest.
Arguments:
- density: float32 [1024, 64, 128], P('gx', 'gz'), may hold values from 1 to 2
- momentum: float32 [3, 1024, 64, 128], P(None, 'gx', 'gz'), may hold values from -1 to 1
- energy: float32 [1024, 64, 128], P('gx', 'gz'), may hold values from 4 to 6
- metric: float32 [1024, 64, 128], P('gx', 'gz'), may hold values from 0.5 to 1.5
- deriv_matrix: float32 [1024, 1024], replicated, may hold values from -0.1875 to 0.1875
- smooth_matrix: float32 [1024, 1024], replicated, may hold values from -0.046875 to 0.046875
- panel_of_cell: int32 [1024, 64], P('gx', 'gz'), may hold values from 0 to 63, as said below
- shape_index: int32 [1024, 64], P('gx', 'gz'), may hold values from 0 to 255
- mode_table: float32 [256, 128], replicated, may hold values from -0.375 to 0.375
Outputs:
- new_density: float32 [1024, 64, 128], P('gx', 'gz')
- new_momentum: float32 [3, 1024, 64, 128], P(None, 'gx', 'gz')
- new_energy: float32 [1024, 64, 128], P('gx', 'gz')
- panel_forces: float32 [64, 128], P('gx')
The draws below stay inside these ranges and needn't reach their ends.
Inputs may be any that keep to these rules, and one draw needn't show every extreme that they name: `panel_of_cell`: each of the 64 panels is one of 8 contiguous uneven runs of streamwise cells times one of 8 contiguous uneven runs of spanwise cells, panel number = run across the span * 8 + run along the stream; every panel has cells.
All inputs are finite; a program needn't handle non-finite values.
Results may differ from the reference program's by a relative error of at most 0.0003.
Values sent between devices are 32-bit elements; how exact they have to be, the bound alone decides.
A program may use at most 128 MiB of HBM per device.

```python
import jax
import jax.numpy as jnp
from jax import lax

NX = 1024
NY = 128
NPX = 8
NPZ = 8
MODES = 128
NSHAPE = 256
NP = 64
NZ = 64


def run_index(key, total, blocks):
    base = total // blocks
    half = base // 2
    delta = jax.random.randint(key, (blocks // 2,), -half, half + 1)
    widths = jnp.stack([base + delta, base - delta], axis=1).reshape(-1)
    ends = jnp.cumsum(widths)
    places = jnp.arange(total)
    return jnp.sum((places[:, None] >= ends[None, :]).astype(jnp.int32), axis=1)


def draw_panel_of_cell(key, part):
    key_x = jax.random.fold_in(key, 11)
    key_z = jax.random.fold_in(key, 23)
    run_x = run_index(key_x, NX, NPX)
    run_z = run_index(key_z, NZ, NPZ)
    return (run_z[None, :] * NPX + run_x[:, None]).astype(jnp.int32)


def set_ends(result, stream_key, low, largest):
    longest = result.shape.index(max(result.shape))
    spots = []
    for shift in (0, 1):
        where = [jax.random.randint(jax.random.fold_in(stream_key, axis), (), 0, length) for axis, length in enumerate(result.shape)]
        where[longest] = (where[longest] + shift) % result.shape[longest]
        spots.append(tuple(where))
    return result.at[spots[0]].set(low).at[spots[1]].set(largest)


def levels(rng, shape, shards, smallest, largest):
    loudness = 1.0
    for axis_at, shards_of in shards:
        draws = jax.random.uniform(jax.random.fold_in(jax.random.fold_in(rng, 6), axis_at), (shards_of,), jnp.float32, smallest / len(shards), largest / len(shards))
        loudness = loudness * jnp.repeat(jnp.exp(draws), shape[axis_at] // shards_of).reshape((-1,) + (1,) * (len(shape) - 1 - axis_at))
    return loudness


def scatter_about(rng, shape, deviation, most, shards=(), dtype=jnp.bfloat16):
    entries = deviation * jax.random.normal(rng, shape, jnp.float32)
    if shards:
        entries = entries * levels(rng, shape, shards, -0.22, 0.18)
    return jnp.clip(entries, -most, most).astype(dtype)


def setup_inputs(seed: int = 0) -> dict:
    seeds = jax.random.split(jax.random.key(seed), 10)
    return {
        "density": jnp.clip(1.0 + 1.0 * jax.random.uniform(seeds[0], (NX, NZ, NY), jnp.float32) ** levels(seeds[0], (NX, NZ, NY), ((0, 8), (1, 4)), -0.2, 0.2), 1.0, 2.0),
        "momentum": scatter_about(seeds[1], (3, NX, NZ, NY), 0.3, 1.0, ((1, 8), (2, 4)), jnp.float32),
        "energy": jnp.clip(4.0 + 2.0 * jax.random.uniform(seeds[2], (NX, NZ, NY), jnp.float32) ** levels(seeds[2], (NX, NZ, NY), ((0, 8), (1, 4)), -0.2, 0.2), 4.0, 6.0),
        "metric": jnp.clip(0.5 + 1.0 * jax.random.uniform(seeds[3], (NX, NZ, NY), jnp.float32) ** levels(seeds[3], (NX, NZ, NY), ((0, 8), (1, 4)), -0.2, 0.2), 0.5, 1.5),
        "deriv_matrix": scatter_about(seeds[4], (NX, NX), NX ** -0.5, 0.1875, (), jnp.float32),
        "smooth_matrix": scatter_about(seeds[5], (NX, NX), (16 * NX) ** -0.5, 0.046875, (), jnp.float32),
        "panel_of_cell": draw_panel_of_cell(jax.random.fold_in(seeds[9], 71), 0),
        "shape_index": set_ends(jax.random.randint(seeds[7], (NX, NZ), 0, NSHAPE), jax.random.fold_in(seeds[7], 1), 0, NSHAPE - 1).astype(jnp.int32),
        "mode_table": scatter_about(seeds[8], (NSHAPE, MODES), NSHAPE ** -0.5, 0.375, (), jnp.float32),
    }


time_step = 0.05
gas_factor = 0.4
pressure_ref = 2.0


def pressure_of(state):
    kinetic = 0.5 * (state[1] * state[1] + state[2] * state[2] + state[3] * state[3]) / state[0]
    return gas_factor * (state[4] - kinetic)


def fluxes(state, direction):
    pressure = pressure_of(state)
    speed = state[1 + direction] / state[0]
    parts = [state[1 + direction]]
    for component in range(3):
        term = state[1 + component] * speed
        if component == direction:
            term = term + pressure
        parts.append(term)
    parts.append((state[4] + pressure) * speed)
    return jnp.stack(parts)


def along_y(field):
    padded = jnp.pad(field, ((0, 0), (0, 0), (0, 0), (2, 2)))
    return (8.0 * (padded[..., 3:-1] - padded[..., 1:-3]) - (padded[..., 4:] - padded[..., :-4])) / 12.0


def along_z(padded):
    return (8.0 * (padded[:, :, 3:-1] - padded[:, :, 1:-3]) - (padded[:, :, 4:] - padded[:, :, :-4])) / 12.0


def x_terms(state, deriv_matrix, smooth_matrix):
    flux = fluxes(state, 0)
    smooth = jnp.einsum('ij,kjzy->kizy', smooth_matrix, state, precision=lax.Precision.HIGHEST)
    slope = jnp.einsum('ij,kjzy->kizy', deriv_matrix, flux, precision=lax.Precision.HIGHEST)
    return smooth - slope


def rate(state, metric, deriv_matrix, smooth_matrix):
    padded = jnp.pad(fluxes(state, 2), ((0, 0), (0, 0), (2, 2), (0, 0)), mode="wrap")
    total = x_terms(state, deriv_matrix, smooth_matrix) - along_y(fluxes(state, 1)) - along_z(padded)
    return metric * total


def reference(density, momentum, energy, metric, deriv_matrix, smooth_matrix, panel_of_cell, shape_index, mode_table):
    state = jnp.concatenate([density[None], momentum, energy[None]], axis=0)
    first = state + time_step * rate(state, metric, deriv_matrix, smooth_matrix)
    final = 0.5 * state + 0.5 * (first + time_step * rate(first, metric, deriv_matrix, smooth_matrix))
    load = (pressure_of(final[:, :, :, 0]) - pressure_ref) * metric[:, :, 0]
    keys = (panel_of_cell * NSHAPE + shape_index).reshape(-1).astype(jnp.int32)
    summed = jax.ops.segment_sum(load.reshape(-1), keys, num_segments=NP * NSHAPE).reshape(NP, NSHAPE)
    forces = jnp.dot(summed, mode_table, precision=lax.Precision.HIGHEST)
    return final[0], final[1:4], final[4], forces
```

```python
import functools

import jax
import jax.numpy as jnp
import numpy as np
from jax import lax
from jax.experimental import pallas as pl
from jax.experimental.pallas import tpu as pltpu
from jax.sharding import PartitionSpec as P

NP = 64

time_step = 0.05
gas_factor = 0.4
pressure_ref = 2.0

F32 = jnp.float32
BF16 = jnp.bfloat16
FIELDS = 5
LANES = 128
EDGE = 32
VMEM = 58 * 1024 * 1024


def params():
    return pltpu.CompilerParams(vmem_limit_bytes=VMEM)


def whole(count):
    return [pl.BlockSpec(memory_space=pltpu.VMEM)] * count


def ring_order(count):
    half = count // 2
    return [2 * p if p < half else 2 * (count - 1 - p) + 1 for p in range(count)]


def pressure_of(state):
    kinetic = 0.5 * (state[1] * state[1] + state[2] * state[2] + state[3] * state[3]) / state[0]
    return gas_factor * (state[4] - kinetic)


def flux_with(state, normal, hits):
    inverse = 1.0 / state[0]
    kinetic = 0.5 * (state[1] * state[1] + state[2] * state[2] + state[3] * state[3]) * inverse
    pressure = gas_factor * (state[4] - kinetic)
    speed = normal * inverse
    parts = [normal]
    for component in range(3):
        term = state[1 + component] * speed
        if hits[component] is True:
            term = term + pressure
        elif hits[component] is not False:
            term = term + jnp.where(hits[component], pressure, 0.0)
        parts.append(term)
    parts.append((state[4] + pressure) * speed)
    return parts


def flux(state, direction):
    return flux_with(state, state[1 + direction], [c == direction for c in range(3)])


def split2(value):
    high = value.astype(BF16)
    return high, (value - high.astype(F32)).astype(BF16)


def split3(value):
    high = value.astype(BF16)
    rest = value - high.astype(F32)
    middle = rest.astype(BF16)
    return high, middle, (rest - middle.astype(F32)).astype(BF16)


def swap_groups(rows, width):
    rows = list(rows)
    count = len(rows)
    shape = rows[0].shape
    axis = len(shape) - 1
    group = lax.broadcasted_iota(jnp.int32, shape, axis) // width
    bit = 1
    while bit < count:
        odd = (group // bit) % 2 == 1
        for k in range(count):
            if k & bit:
                continue
            a, b = rows[k], rows[k | bit]
            rows[k] = jnp.where(odd, pltpu.roll(b, bit * width, axis), a)
            rows[k | bit] = jnp.where(odd, b, pltpu.roll(a, LANES - bit * width, axis))
        bit *= 2
    return rows


def pack_kernel(count, z_cells, order, density, momentum, energy, metric, out):
    x_cells = out.shape[2]
    width = LANES // count
    sources = [density, momentum.at[0], momentum.at[1], momentum.at[2], energy, metric]

    @pl.loop(0, x_cells // 8)
    def _(chunk):
        row = pl.multiple_of(chunk * 8, 8)
        for field, source in enumerate(sources):
            for half in range(z_cells // count):
                planes = [
                    source[pl.ds(row * z_cells + half * count + k, 8, stride=z_cells), :] for k in range(count)
                ]
                tiles = swap_groups(planes, width)
                for t in range(count):
                    out[order[t], field, pl.ds(row, 8), half * LANES : (half + 1) * LANES] = tiles[t]


def unpack_kernel(count, z_cells, order, packed, density, momentum, energy):
    x_cells = packed.shape[2]
    width = LANES // count
    targets = [density, momentum.at[0], momentum.at[1], momentum.at[2], energy]

    @pl.loop(0, x_cells // 8)
    def _(chunk):
        row = pl.multiple_of(chunk * 8, 8)
        for field, target in enumerate(targets):
            for half in range(z_cells // count):
                tiles = [
                    packed[order[t], field, pl.ds(row, 8), half * LANES : (half + 1) * LANES] for t in range(count)
                ]
                planes = swap_groups(tiles, width)
                for k in range(count):
                    target[pl.ds(row * z_cells + half * count + k, 8, stride=z_cells), :] = planes[k]


def matmul_kernel(q, deriv, smooth, out, left_high, left_low, right_high, right_low):
    blocks, _, x_cells, lanes = q.shape
    length = blocks * x_cells

    @pl.loop(0, length // 32)
    def _(chunk):
        row = pl.multiple_of(chunk * 32, 32)
        for column, matrix, sign in ((0, smooth, 1.0), (1, deriv, -1.0)):
            high, low = split2(sign * matrix[pl.ds(row, 32), :])
            left_high[pl.ds(row, 32), column * length : (column + 1) * length] = high
            left_low[pl.ds(row, 32), column * length : (column + 1) * length] = low

    step = 16
    for block in range(blocks):

        @pl.loop(0, x_cells // step)
        def _(chunk):
            row = pl.multiple_of(chunk * step, step)
            state = [q[block, f, pl.ds(row, step), :] for f in range(FIELDS)]
            flow = flux(state, 0)
            for f in range(FIELDS):
                for base, value in ((0, state[f]), (length, flow[f])):
                    high, low = split2(value)
                    at = pl.ds(pl.multiple_of(base + block * x_cells + row, step), step)
                    right_high[f, at, :] = high
                    right_low[f, at, :] = low

    tall = min(512, length)

    @pl.loop(0, length // tall)
    def _(part):
        row = pl.multiple_of(part * tall, tall)

        @pl.loop(0, FIELDS)
        def _(f):
            a = left_high[pl.ds(row, tall), :]
            b = right_high[f]
            total = jnp.dot(a, b, preferred_element_type=F32)
            total += jnp.dot(a, right_low[f], preferred_element_type=F32)
            total += jnp.dot(left_low[pl.ds(row, tall), :], b, preferred_element_type=F32)
            out[f, pl.ds(row, tall), :] = total


def edges_of(values, select):
    return sum(jnp.dot(part, select, preferred_element_type=F32) for part in split3(values))


def rows_of(quarter, row, blocks, x_cells):
    return quarter * (blocks // 4) + row // x_cells, pl.multiple_of(row % x_cells, 16)


def edge_kernel(q, select, out):
    blocks, _, x_cells, lanes = q.shape
    step = 32

    @pl.loop(0, blocks * x_cells // 4 // step)
    def _(chunk):
        row = pl.multiple_of(chunk * step, step)
        for f in range(FIELDS):
            edges = []
            for quarter in range(4):
                block, at = rows_of(quarter, row, blocks, x_cells)
                edges.append(edges_of(q[block, f, pl.ds(at, step), :], select[...]))
            for d, value in enumerate(swap_groups(edges, EDGE)):
                out[d, f, pl.ds(row, step), :] = value


def finish_kernel(second, *refs):
    if second:
        start, q, x_part, h0, h1, h2, h3, mask, weights, out, high, low = refs
        edges_out = None
    else:
        q, x_part, h0, h1, h2, h3, mask, weights, select, out, edges_out, high, low, made = refs
        start = q
    blocks, _, x_cells, lanes = q.shape
    step = 32
    quarter_rows = blocks * x_cells // 4

    @pl.loop(0, quarter_rows // step)
    def _(chunk):
        row = pl.multiple_of(chunk * step, step)
        halo = []
        for f in range(FIELDS):
            halo.append(swap_groups([h[f, pl.ds(row, step), :] for h in (h0, h1, h2, h3)], EDGE))
        lane = lax.broadcasted_iota(jnp.int32, (step, LANES), 1)
        wall = lane < 2 * EDGE
        inside = jnp.broadcast_to(mask[0:1, :], (step, LANES)) > 0.0
        for quarter in range(4):
            block, at = rows_of(quarter, row, blocks, x_cells)
            edge = [halo[f][quarter] for f in range(FIELDS)]
            edge_flux = flux_with(
                edge, jnp.where(wall, edge[2], edge[3]), [False, wall, jnp.logical_not(wall)]
            )
            state = [q[block, f, pl.ds(at, step), :] for f in range(FIELDS)]
            across, along = flux(state, 1), flux(state, 2)
            for f in range(FIELDS):
                base = (quarter * FIELDS + f) * step
                for left, value in (
                    (0, across[f]),
                    (lanes, along[f]),
                    (2 * lanes, jnp.where(inside, edge_flux[f], 0.0)),
                ):
                    top, rest = split2(value)
                    high[base : base + step, left : left + value.shape[1]] = top
                    low[base : base + step, left : left + value.shape[1]] = rest
        slopes = jnp.dot(high[...], weights[...], preferred_element_type=F32)
        slopes += jnp.dot(low[...], weights[...], preferred_element_type=F32)
        for quarter in range(4):
            block, at = rows_of(quarter, row, blocks, x_cells)
            scale = time_step * start[block, FIELDS, pl.ds(at, step), :]
            whole_row = pl.ds(pl.multiple_of(quarter * quarter_rows + row, step), step)
            for f in range(FIELDS):
                base = (quarter * FIELDS + f) * step
                total = x_part[f, whole_row, :] - slopes[base : base + step, :] * (1.0 / 12.0)
                value = q[block, f, pl.ds(at, step), :] + scale * total
                if second:
                    value = 0.5 * start[block, f, pl.ds(at, step), :] + 0.5 * value
                else:
                    made[base : base + step, :] = value
                out[block, f, pl.ds(at, step), :] = value
        if not second:
            edges = edges_of(made[...], select[...])
            for f in range(FIELDS):
                parts = [
                    edges[(r * FIELDS + f) * step : (r * FIELDS + f + 1) * step, :] for r in range(4)
                ]
                for d, value in enumerate(swap_groups(parts, EDGE)):
                    edges_out[d, f, pl.ds(row, step), :] = value


def tables(z_cells, y_cells):
    lanes = z_cells * y_cells
    select = np.zeros((lanes, LANES), np.float32)
    weights = np.zeros((2 * lanes + LANES, lanes), np.float32)
    for c in range(EDGE):
        a, z = (c // z_cells) % 2, c % z_cells
        select[z * y_cells + a, c] = 1
        select[z * y_cells + y_cells - 2 + a, EDGE + c] = 1
        a, y = (c // y_cells) % 2, c % y_cells
        select[a * y_cells + y, 2 * EDGE + c] = 1
        select[(z_cells - 2 + a) * y_cells + y, 3 * EDGE + c] = 1
    halo = 2 * lanes
    for z in range(z_cells):
        for y in range(y_cells):
            to = z * y_cells + y
            for off, factor in ((1, 8.0), (-1, -8.0), (2, -1.0), (-2, 1.0)):
                at = y + off
                if at < 0:
                    source = halo + (at + 2) * z_cells + z
                elif at >= y_cells:
                    source = halo + EDGE + (at - y_cells) * z_cells + z
                else:
                    source = z * y_cells + at
                weights[source, to] += factor
                at = z + off
                if at < 0:
                    source = halo + 2 * EDGE + (at + 2) * y_cells + y
                elif at >= z_cells:
                    source = halo + 3 * EDGE + (at - z_cells) * y_cells + y
                else:
                    source = lanes + at * y_cells + y
                weights[source, to] += factor
    return jnp.asarray(select, BF16), jnp.asarray(weights, BF16)


def exchange(edges, order):
    count = len(order)
    spans = lax.axis_size("gz")
    down = [(order[p], order[(p - 1) % count]) for p in range(count)]
    up = [(order[p], order[(p + 1) % count]) for p in range(count)]
    left = [(i, (i - 1) % spans) for i in range(spans)]
    right = [(i, (i + 1) % spans) for i in range(spans)]
    return (
        lax.ppermute(edges[1], "gx", up),
        lax.ppermute(edges[0], "gx", down),
        lax.ppermute(edges[3], "gz", right),
        lax.ppermute(edges[2], "gz", left),
    )


def cost(flops, moved):
    return pl.CostEstimate(flops=flops, bytes_accessed=moved, transcendentals=0)


def body(
    density,
    momentum,
    energy,
    metric,
    deriv_matrix,
    smooth_matrix,
    panel_of_cell,
    shape_index,
    mode_table,
):
    count = lax.axis_size("gx")
    order = ring_order(count)
    x_cells, z_cells, y_cells = density.shape
    tile_y = y_cells // count
    lanes = z_cells * tile_y
    length = count * x_cells
    flat = (x_cells * z_cells, y_cells)
    select, weights = tables(z_cells, tile_y)

    packed = pl.pallas_call(
        functools.partial(pack_kernel, count, z_cells, order),
        out_shape=jax.ShapeDtypeStruct((count, FIELDS + 1, x_cells, lanes), F32),
        in_specs=whole(4),
        out_specs=whole(1)[0],
        compiler_params=params(),
    )(density.reshape(flat), momentum.reshape((3,) + flat), energy.reshape(flat), metric.reshape(flat))
    start = lax.all_to_all(packed, "gx", split_axis=0, concat_axis=0, tiled=True)

    def x_terms(state):
        return pl.pallas_call(
            matmul_kernel,
            out_shape=jax.ShapeDtypeStruct((FIELDS, length, lanes), F32),
            in_specs=whole(3),
            out_specs=whole(1)[0],
            scratch_shapes=[pltpu.VMEM((length, 2 * length), BF16)] * 2
            + [pltpu.VMEM((FIELDS, 2 * length, lanes), BF16)] * 2,
            compiler_params=params(),
            cost_estimate=cost(12 * FIELDS * length * length * lanes, 40 * FIELDS * length * lanes),
        )(state, deriv_matrix, smooth_matrix)

    edge_shape = jax.ShapeDtypeStruct((4, FIELDS, length // 4, LANES), F32)
    place = jnp.asarray(order, jnp.int32)
    tile = jnp.argmax(place == lax.axis_index("gx"))
    lane = lax.broadcasted_iota(jnp.int32, (8, LANES), 1)
    beyond = ((tile == 0) & (lane < EDGE)) | ((tile == count - 1) & (lane >= EDGE) & (lane < 2 * EDGE))
    mask = jnp.where(beyond, 0.0, 1.0).astype(F32)

    edges = pl.pallas_call(
        edge_kernel,
        out_shape=edge_shape,
        in_specs=whole(2),
        out_specs=whole(1)[0],
        compiler_params=params(),
    )(start, select)
    halo = exchange(edges, order)
    split_rows = [pltpu.VMEM((4 * FIELDS * 32, 2 * lanes + LANES), BF16)] * 2
    first, edges = pl.pallas_call(
        functools.partial(finish_kernel, False),
        out_shape=(jax.ShapeDtypeStruct((count, FIELDS, x_cells, lanes), F32), edge_shape),
        in_specs=whole(9),
        out_specs=tuple(whole(2)),
        scratch_shapes=split_rows + [pltpu.VMEM((4 * FIELDS * 32, lanes), F32)],
        compiler_params=params(),
    )(start, x_terms(start), *halo, mask, weights, select)
    halo = exchange(edges, order)
    final = pl.pallas_call(
        functools.partial(finish_kernel, True),
        out_shape=jax.ShapeDtypeStruct((count, FIELDS, x_cells, lanes), F32),
        in_specs=whole(9),
        out_specs=whole(1)[0],
        scratch_shapes=split_rows,
        compiler_params=params(),
    )(start, first, x_terms(first), *halo, mask, weights)
    back = lax.all_to_all(final, "gx", split_axis=0, concat_axis=0, tiled=True)
    new_density, new_momentum, new_energy = pl.pallas_call(
        functools.partial(unpack_kernel, count, z_cells, order),
        out_shape=(
            jax.ShapeDtypeStruct(flat, F32),
            jax.ShapeDtypeStruct((3,) + flat, F32),
            jax.ShapeDtypeStruct(flat, F32),
        ),
        in_specs=whole(1),
        out_specs=tuple(whole(3)),
        compiler_params=params(),
    )(back)

    floor = back[order[0]].reshape(FIELDS, x_cells, z_cells, tile_y)[..., 0]
    load = ((pressure_of(floor) - pressure_ref) * metric[:, :, 0]).reshape(-1)
    panels = panel_of_cell.reshape(-1)
    shapes = shape_index.reshape(-1)
    shape_hits = (
        shapes[:, None] == jnp.arange(mode_table.shape[0], dtype=jnp.int32)[None, :]
    ).astype(F32)
    panel_hits = (panels[:, None] == jnp.arange(NP, dtype=jnp.int32)[None, :]).astype(F32)
    summed = jnp.dot(panel_hits.T, shape_hits * load[:, None], precision=lax.Precision.HIGHEST)
    partial_forces = jnp.dot(summed, mode_table, precision=lax.Precision.HIGHEST)
    owned = NP // count
    blocks = lax.all_to_all(
        partial_forces.reshape(count, owned, -1), "gx", split_axis=0, concat_axis=0, tiled=True
    )
    spans = lax.axis_size("gz")
    mine = jnp.broadcast_to(jnp.sum(blocks, axis=0)[None], (spans, owned, mode_table.shape[1]))
    forces = jnp.sum(lax.all_to_all(mine, "gz", split_axis=0, concat_axis=0, tiled=True), axis=0)
    return (
        new_density.reshape(density.shape),
        new_momentum.reshape(momentum.shape),
        new_energy.reshape(energy.shape),
        forces,
    )


def solution(mesh):
    in_specs = (
        P("gx", "gz", None),
        P(None, "gx", "gz", None),
        P("gx", "gz", None),
        P("gx", "gz", None),
        P(),
        P(),
        P("gx", "gz"),
        P("gx", "gz"),
        P(),
    )
    out_specs = (P("gx", "gz", None), P(None, "gx", "gz", None), P("gx", "gz", None), P("gx", None))
    return jax.shard_map(body, mesh=mesh, in_specs=in_specs, out_specs=out_specs, check_vma=False)
```

```python
import functools

import jax
import jax.numpy as jnp
import numpy as np
from jax import lax
from jax.experimental import pallas as pl
from jax.experimental.pallas import tpu as pltpu
from jax.sharding import PartitionSpec as P

NP = 64

time_step = 0.05
gas_factor = 0.4
pressure_ref = 2.0

F32 = jnp.float32
BF16 = jnp.bfloat16
FIELDS = 5
LANES = 128
EDGE = 32
VMEM = 58 * 1024 * 1024


def params():
    return pltpu.CompilerParams(vmem_limit_bytes=VMEM)


def whole(count):
    return [pl.BlockSpec(memory_space=pltpu.VMEM)] * count


def ring_order(count):
    half = count // 2
    return [2 * p if p < half else 2 * (count - 1 - p) + 1 for p in range(count)]


def pressure_of(state):
    kinetic = 0.5 * (state[1] * state[1] + state[2] * state[2] + state[3] * state[3]) / state[0]
    return gas_factor * (state[4] - kinetic)


def flux_with(state, normal, hits):
    inverse = 1.0 / state[0]
    kinetic = 0.5 * (state[1] * state[1] + state[2] * state[2] + state[3] * state[3]) * inverse
    pressure = gas_factor * (state[4] - kinetic)
    speed = normal * inverse
    parts = [normal]
    for component in range(3):
        term = state[1 + component] * speed
        if hits[component] is True:
            term = term + pressure
        elif hits[component] is not False:
            term = term + jnp.where(hits[component], pressure, 0.0)
        parts.append(term)
    parts.append((state[4] + pressure) * speed)
    return parts


def flux(state, direction):
    return flux_with(state, state[1 + direction], [c == direction for c in range(3)])


def split2(value):
    high = value.astype(BF16)
    return high, (value - high.astype(F32)).astype(BF16)


def split3(value):
    high = value.astype(BF16)
    rest = value - high.astype(F32)
    middle = rest.astype(BF16)
    return high, middle, (rest - middle.astype(F32)).astype(BF16)


def swap_groups(rows, width):
    rows = list(rows)
    count = len(rows)
    shape = rows[0].shape
    axis = len(shape) - 1
    group = lax.broadcasted_iota(jnp.int32, shape, axis) // width
    bit = 1
    while bit < count:
        odd = (group // bit) % 2 == 1
        for k in range(count):
            if k & bit:
                continue
            a, b = rows[k], rows[k | bit]
            rows[k] = jnp.where(odd, pltpu.roll(b, bit * width, axis), a)
            rows[k | bit] = jnp.where(odd, b, pltpu.roll(a, LANES - bit * width, axis))
        bit *= 2
    return rows


def pack_kernel(count, z_cells, order, *refs):
    out = refs[-1]
    x_cells = out.shape[2]
    width = LANES // count
    sources = refs[:-1]
    if len(sources) == 3:
        density, momentum, energy = sources
        sources = [density, momentum.at[0], momentum.at[1], momentum.at[2], energy]

    @pl.loop(0, x_cells // 8)
    def _(chunk):
        row = pl.multiple_of(chunk * 8, 8)
        for field, source in enumerate(sources):
            for half in range(z_cells // count):
                planes = [
                    source[pl.ds(row * z_cells + half * count + k, 8, stride=z_cells), :] for k in range(count)
                ]
                tiles = swap_groups(planes, width)
                for t in range(count):
                    out[order[t], field, pl.ds(row, 8), half * LANES : (half + 1) * LANES] = tiles[t]


def unpack_kernel(count, z_cells, order, *refs):
    parts, (density, momentum, energy) = refs[:-3], refs[-3:]
    for half, packed in enumerate(parts):
        unpack_part(count, z_cells, order, half * packed.shape[2], packed, density, momentum, energy)


def unpack_part(count, z_cells, order, first_row, packed, density, momentum, energy):
    x_cells = packed.shape[2]
    width = LANES // count
    targets = [density, momentum.at[0], momentum.at[1], momentum.at[2], energy]

    @pl.loop(0, x_cells // 8)
    def _(chunk):
        row = pl.multiple_of(chunk * 8, 8)
        for field, target in enumerate(targets):
            for half in range(z_cells // count):
                tiles = [
                    packed[order[t], field, pl.ds(row, 8), half * LANES : (half + 1) * LANES] for t in range(count)
                ]
                planes = swap_groups(tiles, width)
                for k in range(count):
                    target[pl.ds((first_row + row) * z_cells + half * count + k, 8, stride=z_cells), :] = planes[k]


def matmul_kernel(half, parts, q, deriv, smooth, out, left_high, left_low, right_high, right_low):
    blocks, _, x_cells, lanes = q.shape
    length = blocks * x_cells
    span = x_cells // parts

    @pl.loop(0, length // parts // 32)
    def _(chunk):
        row = pl.multiple_of(chunk * 32, 32)
        source = pl.multiple_of(row // span * x_cells + half * span + row % span, 32)
        for column, matrix, sign in ((0, smooth, 1.0), (1, deriv, -1.0)):
            high, low = split2(sign * matrix[pl.ds(source, 32), :])
            left_high[pl.ds(row, 32), column * length : (column + 1) * length] = high
            left_low[pl.ds(row, 32), column * length : (column + 1) * length] = low

    step = 16
    for block in range(blocks):

        @pl.loop(0, x_cells // step)
        def _(chunk):
            row = pl.multiple_of(chunk * step, step)
            state = [q[block, f, pl.ds(row, step), :] for f in range(FIELDS)]
            flow = flux(state, 0)
            for f in range(FIELDS):
                for base, value in ((0, state[f]), (length, flow[f])):
                    high, low = split2(value)
                    at = pl.ds(pl.multiple_of(base + block * x_cells + row, step), step)
                    right_high[f, at, :] = high
                    right_low[f, at, :] = low

    tall = min(512, length // parts)

    @pl.loop(0, length // parts // tall)
    def _(part):
        row = pl.multiple_of(part * tall, tall)

        @pl.loop(0, FIELDS)
        def _(f):
            a = left_high[pl.ds(row, tall), :]
            b = right_high[f]
            total = jnp.dot(a, b, preferred_element_type=F32)
            total += jnp.dot(a, right_low[f], preferred_element_type=F32)
            total += jnp.dot(left_low[pl.ds(row, tall), :], b, preferred_element_type=F32)
            out[f, pl.ds(row, tall), :] = total


def edges_of(values, select):
    return sum(jnp.dot(part, select, preferred_element_type=F32) for part in split3(values))


def rows_of(quarter, row, blocks, x_cells):
    return quarter * (blocks // 4) + row // x_cells, pl.multiple_of(row % x_cells, 16)


def edge_kernel(q, select, out):
    blocks, _, x_cells, lanes = q.shape
    step = 32

    @pl.loop(0, blocks * x_cells // 4 // step)
    def _(chunk):
        row = pl.multiple_of(chunk * step, step)
        for f in range(FIELDS):
            edges = []
            for quarter in range(4):
                block, at = rows_of(quarter, row, blocks, x_cells)
                edges.append(edges_of(q[block, f, pl.ds(at, step), :], select[...]))
            for d, value in enumerate(swap_groups(edges, EDGE)):
                out[d, f, pl.ds(row, step), :] = value


def finish_kernel(second, half, parts, *refs):
    if second:
        start, metric, q, x_part, h0, h1, h2, h3, mask, weights, out, high, low = refs
        edges_out = None
    else:
        q, metric, x_part, h0, h1, h2, h3, mask, weights, select, out, edges_out, high, low, made = refs
        start = q
    blocks, _, x_cells, lanes = q.shape
    step = 32
    span = x_cells // parts
    quarter_rows = blocks * span // 4

    @pl.loop(0, quarter_rows // step)
    def _(chunk):
        here = pl.multiple_of(chunk * step, step)
        row = pl.multiple_of(here // span * x_cells + half * span + here % span, step)
        kept = pl.multiple_of(here % span, step)
        halo = []
        for f in range(FIELDS):
            halo.append(swap_groups([h[f, pl.ds(row, step), :] for h in (h0, h1, h2, h3)], EDGE))
        lane = lax.broadcasted_iota(jnp.int32, (step, LANES), 1)
        wall = lane < 2 * EDGE
        inside = jnp.broadcast_to(mask[0:1, :], (step, LANES)) > 0.0
        for quarter in range(4):
            block, at = rows_of(quarter, row, blocks, x_cells)
            edge = [halo[f][quarter] for f in range(FIELDS)]
            edge_flux = flux_with(
                edge, jnp.where(wall, edge[2], edge[3]), [False, wall, jnp.logical_not(wall)]
            )
            state = [q[block, f, pl.ds(at, step), :] for f in range(FIELDS)]
            across, along = flux(state, 1), flux(state, 2)
            for f in range(FIELDS):
                base = (quarter * FIELDS + f) * step
                for left, value in (
                    (0, across[f]),
                    (lanes, along[f]),
                    (2 * lanes, jnp.where(inside, edge_flux[f], 0.0)),
                ):
                    top, rest = split2(value)
                    high[base : base + step, left : left + value.shape[1]] = top
                    low[base : base + step, left : left + value.shape[1]] = rest
        slopes = jnp.dot(high[...], weights[...], preferred_element_type=F32)
        slopes += jnp.dot(low[...], weights[...], preferred_element_type=F32)
        for quarter in range(4):
            block, at = rows_of(quarter, row, blocks, x_cells)
            scale = time_step * metric[block, 0, pl.ds(at, step), :]
            whole_row = pl.ds(pl.multiple_of(quarter * quarter_rows + here, step), step)
            for f in range(FIELDS):
                base = (quarter * FIELDS + f) * step
                total = x_part[f, whole_row, :] - slopes[base : base + step, :] * (1.0 / 12.0)
                value = q[block, f, pl.ds(at, step), :] + scale * total
                if second:
                    value = 0.5 * start[block, f, pl.ds(at, step), :] + 0.5 * value
                else:
                    made[base : base + step, :] = value
                out[block, f, pl.ds(kept, step), :] = value
        if not second:
            edges = edges_of(made[...], select[...])
            for f in range(FIELDS):
                parts = [
                    edges[(r * FIELDS + f) * step : (r * FIELDS + f + 1) * step, :] for r in range(4)
                ]
                for d, value in enumerate(swap_groups(parts, EDGE)):
                    edges_out[d, f, pl.ds(row, step), :] = value


def tables(z_cells, y_cells):
    lanes = z_cells * y_cells
    select = np.zeros((lanes, LANES), np.float32)
    weights = np.zeros((2 * lanes + LANES, lanes), np.float32)
    for c in range(EDGE):
        a, z = (c // z_cells) % 2, c % z_cells
        select[z * y_cells + a, c] = 1
        select[z * y_cells + y_cells - 2 + a, EDGE + c] = 1
        a, y = (c // y_cells) % 2, c % y_cells
        select[a * y_cells + y, 2 * EDGE + c] = 1
        select[(z_cells - 2 + a) * y_cells + y, 3 * EDGE + c] = 1
    halo = 2 * lanes
    for z in range(z_cells):
        for y in range(y_cells):
            to = z * y_cells + y
            for off, factor in ((1, 8.0), (-1, -8.0), (2, -1.0), (-2, 1.0)):
                at = y + off
                if at < 0:
                    source = halo + (at + 2) * z_cells + z
                elif at >= y_cells:
                    source = halo + EDGE + (at - y_cells) * z_cells + z
                else:
                    source = z * y_cells + at
                weights[source, to] += factor
                at = z + off
                if at < 0:
                    source = halo + 2 * EDGE + (at + 2) * y_cells + y
                elif at >= z_cells:
                    source = halo + 3 * EDGE + (at - z_cells) * y_cells + y
                else:
                    source = lanes + at * y_cells + y
                weights[source, to] += factor
    return jnp.asarray(select, BF16), jnp.asarray(weights, BF16)


def exchange(edges, order):
    count = len(order)
    spans = lax.axis_size("gz")
    down = [(order[p], order[(p - 1) % count]) for p in range(count)]
    up = [(order[p], order[(p + 1) % count]) for p in range(count)]
    left = [(i, (i - 1) % spans) for i in range(spans)]
    right = [(i, (i + 1) % spans) for i in range(spans)]
    return (
        lax.ppermute(edges[1], "gx", up),
        lax.ppermute(edges[0], "gx", down),
        lax.ppermute(edges[3], "gz", right),
        lax.ppermute(edges[2], "gz", left),
    )


def cost(flops, moved):
    return pl.CostEstimate(flops=flops, bytes_accessed=moved, transcendentals=0)


def body(
    density,
    momentum,
    energy,
    metric,
    deriv_matrix,
    smooth_matrix,
    panel_of_cell,
    shape_index,
    mode_table,
):
    count = lax.axis_size("gx")
    order = ring_order(count)
    x_cells, z_cells, y_cells = density.shape
    tile_y = y_cells // count
    lanes = z_cells * tile_y
    length = count * x_cells
    flat = (x_cells * z_cells, y_cells)
    select, weights = tables(z_cells, tile_y)

    def pack(fields, *arrays):
        return pl.pallas_call(
            functools.partial(pack_kernel, count, z_cells, order),
            out_shape=jax.ShapeDtypeStruct((count, fields, x_cells, lanes), F32),
            in_specs=whole(len(arrays)),
            out_specs=whole(1)[0],
            compiler_params=params(),
        )(*arrays)

    def swap(array):
        return lax.all_to_all(array, "gx", split_axis=0, concat_axis=0, tiled=True)

    start = swap(pack(FIELDS, density.reshape(flat), momentum.reshape((3,) + flat), energy.reshape(flat)))
    packed_metric, start = lax.optimization_barrier((pack(1, metric.reshape(flat)), start))
    tile_metric = swap(packed_metric)

    def x_terms(state, half, parts):
        return pl.pallas_call(
            functools.partial(matmul_kernel, half, parts),
            out_shape=jax.ShapeDtypeStruct((FIELDS, length // parts, lanes), F32),
            in_specs=whole(3),
            out_specs=whole(1)[0],
            scratch_shapes=[pltpu.VMEM((length // parts, 2 * length), BF16)] * 2
            + [pltpu.VMEM((FIELDS, 2 * length, lanes), BF16)] * 2,
            compiler_params=params(),
            cost_estimate=cost(12 * FIELDS * length * length * lanes // parts, 40 * FIELDS * length * lanes),
        )(state, deriv_matrix, smooth_matrix)

    edge_shape = jax.ShapeDtypeStruct((4, FIELDS, length // 4, LANES), F32)
    place = jnp.asarray(order, jnp.int32)
    tile = jnp.argmax(place == lax.axis_index("gx"))
    lane = lax.broadcasted_iota(jnp.int32, (8, LANES), 1)
    beyond = ((tile == 0) & (lane < EDGE)) | ((tile == count - 1) & (lane >= EDGE) & (lane < 2 * EDGE))
    mask = jnp.where(beyond, 0.0, 1.0).astype(F32)

    edges = pl.pallas_call(
        edge_kernel,
        out_shape=edge_shape,
        in_specs=whole(2),
        out_specs=whole(1)[0],
        compiler_params=params(),
    )(start, select)
    halo = exchange(edges, order)
    split_rows = [pltpu.VMEM((4 * FIELDS * 32, 2 * lanes + LANES), BF16)] * 2
    first, edges = pl.pallas_call(
        functools.partial(finish_kernel, False, 0, 1),
        out_shape=(jax.ShapeDtypeStruct((count, FIELDS, x_cells, lanes), F32), edge_shape),
        in_specs=whole(10),
        out_specs=tuple(whole(2)),
        scratch_shapes=split_rows + [pltpu.VMEM((4 * FIELDS * 32, lanes), F32)],
        compiler_params=params(),
    )(start, tile_metric, x_terms(start, 0, 1), *halo, mask, weights, select)
    halo = exchange(edges, order)
    back, parts = [], 1
    for half in range(parts):
        final = pl.pallas_call(
            functools.partial(finish_kernel, True, half, parts),
            out_shape=jax.ShapeDtypeStruct((count, FIELDS, x_cells // parts, lanes), F32),
            in_specs=whole(10),
            out_specs=whole(1)[0],
            scratch_shapes=split_rows,
            compiler_params=params(),
            cost_estimate=cost(10**10, 40 * FIELDS * length * lanes // parts),
        )(start, tile_metric, first, x_terms(first, half, parts), *halo, mask, weights)
        final, first = lax.optimization_barrier((final, first))
        back.append(swap(final))
    new_density, new_momentum, new_energy = pl.pallas_call(
        functools.partial(unpack_kernel, count, z_cells, order),
        out_shape=(
            jax.ShapeDtypeStruct(flat, F32),
            jax.ShapeDtypeStruct((3,) + flat, F32),
            jax.ShapeDtypeStruct(flat, F32),
        ),
        in_specs=whole(parts),
        out_specs=tuple(whole(3)),
        compiler_params=params(),
    )(*back)

    floor = jnp.concatenate([part[order[0]] for part in back], axis=1).reshape(FIELDS, x_cells, z_cells, tile_y)[..., 0]
    load = ((pressure_of(floor) - pressure_ref) * metric[:, :, 0]).reshape(-1)
    panels = panel_of_cell.reshape(-1)
    shapes = shape_index.reshape(-1)
    shape_hits = (
        shapes[:, None] == jnp.arange(mode_table.shape[0], dtype=jnp.int32)[None, :]
    ).astype(F32)
    panel_hits = (panels[:, None] == jnp.arange(NP, dtype=jnp.int32)[None, :]).astype(F32)
    summed = jnp.dot(panel_hits.T, shape_hits * load[:, None], precision=lax.Precision.HIGHEST)
    partial_forces = jnp.dot(summed, mode_table, precision=lax.Precision.HIGHEST)
    owned = NP // count
    blocks = lax.all_to_all(
        partial_forces.reshape(count, owned, -1), "gx", split_axis=0, concat_axis=0, tiled=True
    )
    spans = lax.axis_size("gz")
    mine = jnp.broadcast_to(jnp.sum(blocks, axis=0)[None], (spans, owned, mode_table.shape[1]))
    forces = jnp.sum(lax.all_to_all(mine, "gz", split_axis=0, concat_axis=0, tiled=True), axis=0)
    return (
        new_density.reshape(density.shape),
        new_momentum.reshape(momentum.shape),
        new_energy.reshape(energy.shape),
        forces,
    )


def solution(mesh):
    in_specs = (
        P("gx", "gz", None),
        P(None, "gx", "gz", None),
        P("gx", "gz", None),
        P("gx", "gz", None),
        P(),
        P(),
        P("gx", "gz"),
        P("gx", "gz"),
        P(),
    )
    out_specs = (P("gx", "gz", None), P(None, "gx", "gz", None), P("gx", "gz", None), P("gx", None))
    return jax.shard_map(body, mesh=mesh, in_specs=in_specs, out_specs=out_specs, check_vma=False)
```

```python
import functools

import jax
import jax.numpy as jnp
import numpy as np
from jax import lax
from jax.experimental import pallas as pl
from jax.experimental.pallas import tpu as pltpu
from jax.sharding import PartitionSpec as P

NP = 64

time_step = 0.05
gas_factor = 0.4
pressure_ref = 2.0

F32 = jnp.float32
BF16 = jnp.bfloat16
FIELDS = 5
LANES = 128
EDGE = 32
VMEM = 58 * 1024 * 1024


def params():
    return pltpu.CompilerParams(vmem_limit_bytes=VMEM)


def whole(count):
    return [pl.BlockSpec(memory_space=pltpu.VMEM)] * count


def ring_order(count):
    half = count // 2
    return [2 * p if p < half else 2 * (count - 1 - p) + 1 for p in range(count)]


def pressure_of(state):
    kinetic = 0.5 * (state[1] * state[1] + state[2] * state[2] + state[3] * state[3]) / state[0]
    return gas_factor * (state[4] - kinetic)


def flux_with(state, normal, hits):
    inverse = 1.0 / state[0]
    kinetic = 0.5 * (state[1] * state[1] + state[2] * state[2] + state[3] * state[3]) * inverse
    pressure = gas_factor * (state[4] - kinetic)
    speed = normal * inverse
    parts = [normal]
    for component in range(3):
        term = state[1 + component] * speed
        if hits[component] is True:
            term = term + pressure
        elif hits[component] is not False:
            term = term + jnp.where(hits[component], pressure, 0.0)
        parts.append(term)
    parts.append((state[4] + pressure) * speed)
    return parts


def flux(state, direction):
    return flux_with(state, state[1 + direction], [c == direction for c in range(3)])


def split2(value):
    high = value.astype(BF16)
    return high, (value - high.astype(F32)).astype(BF16)


def split3(value):
    high = value.astype(BF16)
    rest = value - high.astype(F32)
    middle = rest.astype(BF16)
    return high, middle, (rest - middle.astype(F32)).astype(BF16)


def swap_groups(rows, width):
    rows = list(rows)
    count = len(rows)
    shape = rows[0].shape
    axis = len(shape) - 1
    group = lax.broadcasted_iota(jnp.int32, shape, axis) // width
    bit = 1
    while bit < count:
        odd = (group // bit) % 2 == 1
        for k in range(count):
            if k & bit:
                continue
            a, b = rows[k], rows[k | bit]
            rows[k] = jnp.where(odd, pltpu.roll(b, bit * width, axis), a)
            rows[k | bit] = jnp.where(odd, b, pltpu.roll(a, LANES - bit * width, axis))
        bit *= 2
    return rows


def pack_kernel(count, z_cells, order, *refs):
    out = refs[-1]
    x_cells = out.shape[2]
    width = LANES // count
    sources = refs[:-1]
    if len(sources) == 3:
        density, momentum, energy = sources
        sources = [density, momentum.at[0], momentum.at[1], momentum.at[2], energy]

    @pl.loop(0, x_cells // 8)
    def _(chunk):
        row = pl.multiple_of(chunk * 8, 8)
        for field, source in enumerate(sources):
            for half in range(z_cells // count):
                planes = [
                    source[pl.ds(row * z_cells + half * count + k, 8, stride=z_cells), :] for k in range(count)
                ]
                tiles = swap_groups(planes, width)
                for t in range(count):
                    out[order[t], field, pl.ds(row, 8), half * LANES : (half + 1) * LANES] = tiles[t]


def unpack_kernel(count, z_cells, order, *refs):
    parts, (density, momentum, energy) = refs[:-3], refs[-3:]
    for half, packed in enumerate(parts):
        unpack_part(count, z_cells, order, half * packed.shape[2], packed, density, momentum, energy)


def unpack_part(count, z_cells, order, first_row, packed, density, momentum, energy):
    x_cells = packed.shape[2]
    width = LANES // count
    targets = [density, momentum.at[0], momentum.at[1], momentum.at[2], energy]

    @pl.loop(0, x_cells // 8)
    def _(chunk):
        row = pl.multiple_of(chunk * 8, 8)
        for field, target in enumerate(targets):
            for half in range(z_cells // count):
                tiles = [
                    packed[order[t], field, pl.ds(row, 8), half * LANES : (half + 1) * LANES] for t in range(count)
                ]
                planes = swap_groups(tiles, width)
                for k in range(count):
                    target[pl.ds((first_row + row) * z_cells + half * count + k, 8, stride=z_cells), :] = planes[k]


def matrices_kernel(deriv, smooth, left_high, left_low):
    length = deriv.shape[0]

    @pl.loop(0, length // 32)
    def _(chunk):
        row = pl.multiple_of(chunk * 32, 32)
        for column, matrix, sign in ((0, smooth, 1.0), (1, deriv, -1.0)):
            high, low = split2(sign * matrix[pl.ds(row, 32), :])
            left_high[pl.ds(row, 32), column * length : (column + 1) * length] = high
            left_low[pl.ds(row, 32), column * length : (column + 1) * length] = low


def matmul_kernel(parts, q, left_high, left_low, out, right_high, right_low):
    blocks, _, x_cells, lanes = q.shape
    length = blocks * x_cells
    step = 16
    for block in range(blocks):

        @pl.loop(0, x_cells // step)
        def _(chunk):
            row = pl.multiple_of(chunk * step, step)
            state = [q[block, f, pl.ds(row, step), :] for f in range(FIELDS)]
            flow = flux(state, 0)
            for f in range(FIELDS):
                for base, value in ((0, state[f]), (length, flow[f])):
                    high, low = split2(value)
                    at = pl.ds(pl.multiple_of(base + block * x_cells + row, step), step)
                    right_high[f, at, :] = high
                    right_low[f, at, :] = low

    tall = min(512, length // parts)

    @pl.loop(0, length // parts // tall)
    def _(part):
        row = pl.multiple_of(part * tall, tall)

        @pl.loop(0, FIELDS)
        def _(f):
            a = left_high[pl.ds(row, tall), :]
            b = right_high[f]
            total = jnp.dot(a, b, preferred_element_type=F32)
            total += jnp.dot(a, right_low[f], preferred_element_type=F32)
            total += jnp.dot(left_low[pl.ds(row, tall), :], b, preferred_element_type=F32)
            out[f, pl.ds(row, tall), :] = total


def edges_of(values, select):
    return sum(jnp.dot(part, select, preferred_element_type=F32) for part in split3(values))


def rows_of(quarter, row, blocks, x_cells):
    return quarter * (blocks // 4) + row // x_cells, pl.multiple_of(row % x_cells, 16)


def edge_kernel(q, select, out):
    blocks, _, x_cells, lanes = q.shape
    step = 32

    @pl.loop(0, blocks * x_cells // 4 // step)
    def _(chunk):
        row = pl.multiple_of(chunk * step, step)
        for f in range(FIELDS):
            edges = []
            for quarter in range(4):
                block, at = rows_of(quarter, row, blocks, x_cells)
                edges.append(edges_of(q[block, f, pl.ds(at, step), :], select[...]))
            for d, value in enumerate(swap_groups(edges, EDGE)):
                out[d, f, pl.ds(row, step), :] = value


def finish_kernel(second, half, parts, *refs):
    if second:
        start, metric, q, x_part, h0, h1, h2, h3, mask, weights, out, high, low = refs
        edges_out = None
    else:
        q, metric, x_part, h0, h1, h2, h3, mask, weights, select, out, edges_out, high, low, made = refs
        start = q
    blocks, _, x_cells, lanes = q.shape
    step = 32
    span = x_cells // parts
    quarter_rows = blocks * span // 4

    @pl.loop(0, quarter_rows // step)
    def _(chunk):
        here = pl.multiple_of(chunk * step, step)
        row = pl.multiple_of(here // span * x_cells + half * span + here % span, step)
        kept = pl.multiple_of(here % span, step)
        halo = []
        for f in range(FIELDS):
            halo.append(swap_groups([h[f, pl.ds(row, step), :] for h in (h0, h1, h2, h3)], EDGE))
        lane = lax.broadcasted_iota(jnp.int32, (step, LANES), 1)
        wall = lane < 2 * EDGE
        inside = jnp.broadcast_to(mask[0:1, :], (step, LANES)) > 0.0
        for quarter in range(4):
            block, at = rows_of(quarter, row, blocks, x_cells)
            edge = [halo[f][quarter] for f in range(FIELDS)]
            edge_flux = flux_with(
                edge, jnp.where(wall, edge[2], edge[3]), [False, wall, jnp.logical_not(wall)]
            )
            state = [q[block, f, pl.ds(at, step), :] for f in range(FIELDS)]
            across, along = flux(state, 1), flux(state, 2)
            for f in range(FIELDS):
                base = (quarter * FIELDS + f) * step
                for left, value in (
                    (0, across[f]),
                    (lanes, along[f]),
                    (2 * lanes, jnp.where(inside, edge_flux[f], 0.0)),
                ):
                    top, rest = split2(value)
                    high[base : base + step, left : left + value.shape[1]] = top
                    low[base : base + step, left : left + value.shape[1]] = rest
        slopes = jnp.dot(high[...], weights[...], preferred_element_type=F32)
        slopes += jnp.dot(low[...], weights[...], preferred_element_type=F32)
        for quarter in range(4):
            block, at = rows_of(quarter, row, blocks, x_cells)
            scale = time_step * metric[block, 0, pl.ds(at, step), :]
            whole_row = pl.ds(pl.multiple_of(quarter * quarter_rows + here, step), step)
            for f in range(FIELDS):
                base = (quarter * FIELDS + f) * step
                total = x_part[f, whole_row, :] - slopes[base : base + step, :] * (1.0 / 12.0)
                value = q[block, f, pl.ds(at, step), :] + scale * total
                if second:
                    value = 0.5 * start[block, f, pl.ds(at, step), :] + 0.5 * value
                else:
                    made[base : base + step, :] = value
                out[block, f, pl.ds(kept, step), :] = value
        if not second:
            edges = edges_of(made[...], select[...])
            for f in range(FIELDS):
                parts = [
                    edges[(r * FIELDS + f) * step : (r * FIELDS + f + 1) * step, :] for r in range(4)
                ]
                for d, value in enumerate(swap_groups(parts, EDGE)):
                    edges_out[d, f, pl.ds(row, step), :] = value


def tables(z_cells, y_cells):
    lanes = z_cells * y_cells
    select = np.zeros((lanes, LANES), np.float32)
    weights = np.zeros((2 * lanes + LANES, lanes), np.float32)
    for c in range(EDGE):
        a, z = (c // z_cells) % 2, c % z_cells
        select[z * y_cells + a, c] = 1
        select[z * y_cells + y_cells - 2 + a, EDGE + c] = 1
        a, y = (c // y_cells) % 2, c % y_cells
        select[a * y_cells + y, 2 * EDGE + c] = 1
        select[(z_cells - 2 + a) * y_cells + y, 3 * EDGE + c] = 1
    halo = 2 * lanes
    for z in range(z_cells):
        for y in range(y_cells):
            to = z * y_cells + y
            for off, factor in ((1, 8.0), (-1, -8.0), (2, -1.0), (-2, 1.0)):
                at = y + off
                if at < 0:
                    source = halo + (at + 2) * z_cells + z
                elif at >= y_cells:
                    source = halo + EDGE + (at - y_cells) * z_cells + z
                else:
                    source = z * y_cells + at
                weights[source, to] += factor
                at = z + off
                if at < 0:
                    source = halo + 2 * EDGE + (at + 2) * y_cells + y
                elif at >= z_cells:
                    source = halo + 3 * EDGE + (at - z_cells) * y_cells + y
                else:
                    source = lanes + at * y_cells + y
                weights[source, to] += factor
    return jnp.asarray(select, BF16), jnp.asarray(weights, BF16)


def exchange(edges, order):
    count = len(order)
    spans = lax.axis_size("gz")
    down = [(order[p], order[(p - 1) % count]) for p in range(count)]
    up = [(order[p], order[(p + 1) % count]) for p in range(count)]
    left = [(i, (i - 1) % spans) for i in range(spans)]
    right = [(i, (i + 1) % spans) for i in range(spans)]
    return (
        lax.ppermute(edges[1], "gx", up),
        lax.ppermute(edges[0], "gx", down),
        lax.ppermute(edges[3], "gz", right),
        lax.ppermute(edges[2], "gz", left),
    )


def cost(flops, moved):
    return pl.CostEstimate(flops=flops, bytes_accessed=moved, transcendentals=0)


def body(
    density,
    momentum,
    energy,
    metric,
    deriv_matrix,
    smooth_matrix,
    panel_of_cell,
    shape_index,
    mode_table,
):
    count = lax.axis_size("gx")
    order = ring_order(count)
    x_cells, z_cells, y_cells = density.shape
    tile_y = y_cells // count
    lanes = z_cells * tile_y
    length = count * x_cells
    flat = (x_cells * z_cells, y_cells)
    select, weights = tables(z_cells, tile_y)

    def pack(fields, *arrays):
        return pl.pallas_call(
            functools.partial(pack_kernel, count, z_cells, order),
            out_shape=jax.ShapeDtypeStruct((count, fields, x_cells, lanes), F32),
            in_specs=whole(len(arrays)),
            out_specs=whole(1)[0],
            compiler_params=params(),
        )(*arrays)

    def swap(array):
        return lax.all_to_all(array, "gx", split_axis=0, concat_axis=0, tiled=True)

    start = swap(pack(FIELDS, density.reshape(flat), momentum.reshape((3,) + flat), energy.reshape(flat)))
    left_high, left_low = pl.pallas_call(
        matrices_kernel,
        out_shape=(jax.ShapeDtypeStruct((length, 2 * length), BF16),) * 2,
        in_specs=whole(2),
        out_specs=tuple(whole(2)),
        compiler_params=params(),
    )(deriv_matrix, smooth_matrix)
    packed_metric, left_high, left_low, start = lax.optimization_barrier(
        (pack(1, metric.reshape(flat)), left_high, left_low, start)
    )
    tile_metric = swap(packed_metric)

    def x_terms(state, half, parts):
        return pl.pallas_call(
            functools.partial(matmul_kernel, parts),
            out_shape=jax.ShapeDtypeStruct((FIELDS, length // parts, lanes), F32),
            in_specs=whole(3),
            out_specs=whole(1)[0],
            scratch_shapes=[pltpu.VMEM((FIELDS, 2 * length, lanes), BF16)] * 2,
            compiler_params=params(),
            cost_estimate=cost(12 * FIELDS * length * length * lanes // parts, 40 * FIELDS * length * lanes),
        )(state, left_high, left_low)

    edge_shape = jax.ShapeDtypeStruct((4, FIELDS, length // 4, LANES), F32)
    place = jnp.asarray(order, jnp.int32)
    tile = jnp.argmax(place == lax.axis_index("gx"))
    lane = lax.broadcasted_iota(jnp.int32, (8, LANES), 1)
    beyond = ((tile == 0) & (lane < EDGE)) | ((tile == count - 1) & (lane >= EDGE) & (lane < 2 * EDGE))
    mask = jnp.where(beyond, 0.0, 1.0).astype(F32)

    edges = pl.pallas_call(
        edge_kernel,
        out_shape=edge_shape,
        in_specs=whole(2),
        out_specs=whole(1)[0],
        compiler_params=params(),
    )(start, select)
    halo = exchange(edges, order)
    split_rows = [pltpu.VMEM((4 * FIELDS * 32, 2 * lanes + LANES), BF16)] * 2
    first, edges = pl.pallas_call(
        functools.partial(finish_kernel, False, 0, 1),
        out_shape=(jax.ShapeDtypeStruct((count, FIELDS, x_cells, lanes), F32), edge_shape),
        in_specs=whole(10),
        out_specs=tuple(whole(2)),
        scratch_shapes=split_rows + [pltpu.VMEM((4 * FIELDS * 32, lanes), F32)],
        compiler_params=params(),
    )(start, tile_metric, x_terms(start, 0, 1), *halo, mask, weights, select)
    halo = exchange(edges, order)
    back, parts = [], 1
    for half in range(parts):
        final = pl.pallas_call(
            functools.partial(finish_kernel, True, half, parts),
            out_shape=jax.ShapeDtypeStruct((count, FIELDS, x_cells // parts, lanes), F32),
            in_specs=whole(10),
            out_specs=whole(1)[0],
            scratch_shapes=split_rows,
            compiler_params=params(),
            cost_estimate=cost(10**10, 40 * FIELDS * length * lanes // parts),
        )(start, tile_metric, first, x_terms(first, half, parts), *halo, mask, weights)
        final, first = lax.optimization_barrier((final, first))
        back.append(swap(final))
    new_density, new_momentum, new_energy = pl.pallas_call(
        functools.partial(unpack_kernel, count, z_cells, order),
        out_shape=(
            jax.ShapeDtypeStruct(flat, F32),
            jax.ShapeDtypeStruct((3,) + flat, F32),
            jax.ShapeDtypeStruct(flat, F32),
        ),
        in_specs=whole(parts),
        out_specs=tuple(whole(3)),
        compiler_params=params(),
    )(*back)

    floor = jnp.concatenate([part[order[0]] for part in back], axis=1).reshape(FIELDS, x_cells, z_cells, tile_y)[..., 0]
    load = ((pressure_of(floor) - pressure_ref) * metric[:, :, 0]).reshape(-1)
    panels = panel_of_cell.reshape(-1)
    shapes = shape_index.reshape(-1)
    shape_hits = (
        shapes[:, None] == jnp.arange(mode_table.shape[0], dtype=jnp.int32)[None, :]
    ).astype(F32)
    panel_hits = (panels[:, None] == jnp.arange(NP, dtype=jnp.int32)[None, :]).astype(F32)
    summed = jnp.dot(panel_hits.T, shape_hits * load[:, None], precision=lax.Precision.HIGHEST)
    partial_forces = jnp.dot(summed, mode_table, precision=lax.Precision.HIGHEST)
    owned = NP // count
    blocks = lax.all_to_all(
        partial_forces.reshape(count, owned, -1), "gx", split_axis=0, concat_axis=0, tiled=True
    )
    spans = lax.axis_size("gz")
    mine = jnp.broadcast_to(jnp.sum(blocks, axis=0)[None], (spans, owned, mode_table.shape[1]))
    forces = jnp.sum(lax.all_to_all(mine, "gz", split_axis=0, concat_axis=0, tiled=True), axis=0)
    return (
        new_density.reshape(density.shape),
        new_momentum.reshape(momentum.shape),
        new_energy.reshape(energy.shape),
        forces,
    )


def solution(mesh):
    in_specs = (
        P("gx", "gz", None),
        P(None, "gx", "gz", None),
        P("gx", "gz", None),
        P("gx", "gz", None),
        P(),
        P(),
        P("gx", "gz"),
        P("gx", "gz"),
        P(),
    )
    out_specs = (P("gx", "gz", None), P(None, "gx", "gz", None), P("gx", "gz", None), P("gx", None))
    return jax.shard_map(body, mesh=mesh, in_specs=in_specs, out_specs=out_specs, check_vma=False)
```
